32 devices in a mesh: group: 2 (over x), row: 8 (over z, y), col: 2 (over core).
Axes of the slice: x: 2, y: 2, z: 4, core: 2. Of those that a mesh axis runs over, the one named last changes fastest.
Arguments:
- homolog_features: bfloat16 [1024, 3072], P(('group', 'row')), parts along dimension 0, may hold values from -6 to 6
- normalizer_factor: float32 [64], replicated, may hold values from 0.5 to 1.5
- normalizer_shift: float32 [64], replicated, may hold values from -3 to 3
- first_weights_table: bfloat16 [64, 32], replicated, may hold values from -0.75 to 0.75
- second_weights_table: bfloat16 [64, 32], replicated, may hold values from -0.75 to 0.75
- output_matrix: bfloat16 [1024, 128], replicated, may hold values from -1.796875 to 1.796875
- output_bias: float32 [128], replicated, may hold values from -6 to 6
- pair_update_cotangent: bfloat16 [1024, 512, 128], P(('group', 'row'), 'col'), parts along dimension 0, may hold values from -1.796875 to 1.796875
Outputs:
- pair_delta: bfloat16 [1024, 512, 128], P(('group', 'row'), 'col'), parts along dimension 0
- alignment_gradient: bfloat16 [1024, 3072], P(('group', 'row')), parts along dimension 0
The draws below stay inside these ranges and needn't reach their ends.
There are 2 independent parts, one for each index of `group`. The reference program is written for one: setup_inputs(seed, part) draws one part's arguments, and reference() takes and returns one part's arrays. A program takes and returns all parts, laid end to end along the dimension named above; an argument that names none is the same for every part. Nothing has to cross between parts.
All inputs are finite; a program needn't handle non-finite values.
Results may differ from the reference program's by a relative error of at most 0.0064.
Values may be sent and summed in bfloat16 or wider, within the bound.
A program may use at most 192 MiB of HBM per device.

```python
import jax
import jax.numpy as jnp
from jax import lax

HOMOLOG_TOTAL = 48
FEATURE_WIDTH = 64
HIDDEN_WIDTH = 32
CZ = 128
CHAIN_LENGTH = 512


def level_of(rng, dims, shards, low, largest):
    loudness = 1.0
    for axis_at, shards_of in shards:
        heights = jax.random.uniform(jax.random.fold_in(jax.random.fold_in(rng, 6), axis_at), (shards_of,), jnp.float32, low / len(shards), largest / len(shards))
        loudness = loudness * jnp.repeat(jnp.exp(heights), dims[axis_at] // shards_of).reshape((-1,) + (1,) * (len(dims) - 1 - axis_at))
    return loudness


def scatter_about(own_key, dims, deviation, limit, pieces=(), kind=jnp.bfloat16):
    values = deviation * jax.random.normal(own_key, dims, jnp.float32)
    if pieces:
        values = values * level_of(own_key, dims, pieces, -0.22, 0.18)
    return jnp.clip(values, -limit, limit).astype(kind)


def setup_inputs(seed: int = 0, part: int = 0) -> dict:
    key_of = jax.random.split(jax.random.key(seed), 9)
    part_keys = jax.random.split(jax.random.fold_in(key_of[8], part), 9)
    return {
        "homolog_features": scatter_about(part_keys[0], (CHAIN_LENGTH, HOMOLOG_TOTAL * FEATURE_WIDTH), 1.0, 6.0, ((0, 8),)),
        "normalizer_factor": jnp.clip(1.0 + 0.1 * jax.random.normal(key_of[1], (FEATURE_WIDTH,), jnp.float32), 0.5, 1.5),
        "normalizer_shift": scatter_about(key_of[2], (FEATURE_WIDTH,), 0.5, 3.0, (), jnp.float32),
        "first_weights_table": scatter_about(key_of[3], (FEATURE_WIDTH, HIDDEN_WIDTH), FEATURE_WIDTH ** -0.5, 0.75),
        "second_weights_table": scatter_about(key_of[4], (FEATURE_WIDTH, HIDDEN_WIDTH), FEATURE_WIDTH ** -0.5, 0.75),
        "output_matrix": scatter_about(key_of[5], (HIDDEN_WIDTH * HIDDEN_WIDTH, CZ), 0.3, 1.796875),
        "output_bias": scatter_about(key_of[6], (CZ,), 1.0, 6.0, (), jnp.float32),
        "pair_update_cotangent": scatter_about(part_keys[7], (CHAIN_LENGTH, CHAIN_LENGTH, CZ), 0.3, 1.796875, ((0, 8), (1, 2))),
    }


def apply_layer_norm(homolog_features, normalizer_factor, normalizer_shift):
    entry_number = homolog_features.shape[0]
    quantity_tensor = homolog_features.astype(jnp.float32).reshape(entry_number, HOMOLOG_TOTAL, FEATURE_WIDTH)
    center = quantity_tensor - lax.optimization_barrier(jnp.mean(quantity_tensor, axis=-1, keepdims=True))
    inverse_scale = lax.rsqrt(lax.optimization_barrier(jnp.mean(center * center, axis=-1, keepdims=True)) + 1e-05)
    standard_deviation = center * inverse_scale
    normalized_block = (standard_deviation * normalizer_factor + normalizer_shift).astype(jnp.bfloat16)
    return (normalized_block, standard_deviation, inverse_scale)

def project(normalized_block, weight):
    return jnp.einsum('isc,ch->ihs', normalized_block.astype(jnp.float32), weight.astype(jnp.float32)).astype(jnp.bfloat16)

def input_gradient(left_gradient, right_gradient, standard_deviation, inverse_scale, normalizer_factor, first_weights_table, second_weights_table):
    highest = lax.Precision.HIGHEST
    dnormed = jnp.einsum('ihs,ch->isc', left_gradient, first_weights_table.astype(jnp.float32), precision=highest)
    dnormed = dnormed + jnp.einsum('ihs,ch->isc', right_gradient, second_weights_table.astype(jnp.float32), precision=highest)
    scaled = dnormed * normalizer_factor
    result = inverse_scale * (scaled - lax.optimization_barrier(jnp.mean(scaled, axis=-1, keepdims=True)) - standard_deviation * lax.optimization_barrier(jnp.mean(scaled * standard_deviation, axis=-1, keepdims=True)))
    return result.reshape(result.shape[0], -1).astype(jnp.bfloat16)

def reference(homolog_features, normalizer_factor, normalizer_shift, first_weights_table, second_weights_table, output_matrix, output_bias, pair_update_cotangent):
    normalized_block, standard_deviation, inverse_scale = apply_layer_norm(homolog_features, normalizer_factor, normalizer_shift)
    left_proj = project(normalized_block, first_weights_table)
    right_proj = project(normalized_block, second_weights_table)
    residues = left_proj.shape[0]
    right_flat = right_proj.reshape(residues * HIDDEN_WIDTH, HOMOLOG_TOTAL)
    weight_three = output_matrix.astype(jnp.float32).reshape(HIDDEN_WIDTH, HIDDEN_WIDTH, CZ)
    block_rows = 16
    block_count = residues // block_rows

    def advance(running, inputs):
        left_block, cot_block = inputs
        left_flat = left_block.reshape(block_rows * HIDDEN_WIDTH, HOMOLOG_TOTAL)
        outer = lax.dot_general(left_flat, right_flat, (((1,), (1,)), ((), ())), preferred_element_type=jnp.float32) / HOMOLOG_TOTAL
        outer = outer.astype(jnp.bfloat16).reshape(block_rows, HIDDEN_WIDTH, residues, HIDDEN_WIDTH)
        update = jnp.einsum('iajb,abk->ijk', outer.astype(jnp.float32), weight_three) + output_bias
        update = update.astype(jnp.bfloat16)
        grad_outer = jnp.einsum('ijk,abk->iajb', cot_block.astype(jnp.float32), weight_three).astype(jnp.bfloat16)
        grad_flat = grad_outer.reshape(block_rows * HIDDEN_WIDTH, residues * HIDDEN_WIDTH)
        left_part = jnp.dot(grad_flat, right_flat, preferred_element_type=jnp.float32) / HOMOLOG_TOTAL
        right_part = lax.dot_general(grad_flat, left_flat, (((0,), (0,)), ((), ())), preferred_element_type=jnp.float32) / HOMOLOG_TOTAL
        return (running + right_part, (update, left_part.reshape(block_rows, HIDDEN_WIDTH, HOMOLOG_TOTAL)))
    zero_sums = jnp.zeros((residues * HIDDEN_WIDTH, HOMOLOG_TOTAL), jnp.float32)
    right_sum, (updates, left_parts) = lax.scan(advance, zero_sums, (left_proj.reshape(block_count, block_rows, HIDDEN_WIDTH, HOMOLOG_TOTAL), pair_update_cotangent.reshape(block_count, block_rows, residues, CZ)))
    pair_delta = updates.reshape(residues, residues, CZ)
    left_gradient = left_parts.reshape(residues, HIDDEN_WIDTH, HOMOLOG_TOTAL)
    right_gradient = right_sum.reshape(residues, HIDDEN_WIDTH, HOMOLOG_TOTAL)
    alignment_gradient = input_gradient(left_gradient, right_gradient, standard_deviation, inverse_scale, normalizer_factor, first_weights_table, second_weights_table)
    return (pair_delta, alignment_gradient)
```

```python
import functools

import jax
import jax.numpy as jnp
from jax import lax
from jax.experimental import pallas as pl
from jax.experimental.pallas import tpu as pltpu
from jax.sharding import PartitionSpec as P

SEQS = 48
CHANNELS = 64
HIDDEN = 32
BLOCK = 8


def pair_kernel(left_ref, right_ref, w_ref, wt_ref, bias_ref, cot_ref,
                out_ref, lg_ref, rg_ref, right_t, z, v, cots, total):
    step = pl.program_id(0)
    cols = right_ref.shape[0]
    cz = cot_ref.shape[2]
    scale = 1.0 / SEQS

    @pl.when(step == 0)
    def _():
        right_t[...] = right_ref[...].T
        total[...] = jnp.zeros_like(total)

    for i in range(BLOCK):
        cots[:, i * cz:(i + 1) * cz] = cot_ref[i]

    group = 4

    @pl.loop(0, HIDDEN // group)
    def _(g):
        lanes = pl.ds(pl.multiple_of(g * group * cz, group * cz), group * cz)
        part = jnp.dot(left_ref[...], w_ref[:, lanes],
                       preferred_element_type=jnp.float32).astype(jnp.bfloat16)
        for b in range(group):
            for i in range(BLOCK):
                rows = pl.ds(pl.multiple_of((g * group + b) * SEQS, 16), SEQS)
                z[rows, i * cz:(i + 1) * cz] = part[
                    i * SEQS:(i + 1) * SEQS, b * cz:(b + 1) * cz]

    @pl.loop(0, BLOCK // 2)
    def _(p):
        lanes = pl.ds(pl.multiple_of(p * 2 * cz, 2 * cz), 2 * cz)
        res = jnp.dot(right_ref[...], z[:, lanes],
                      preferred_element_type=jnp.float32) * scale
        for q in range(2):
            out_ref[2 * p + q] = (res[:, q * cz:(q + 1) * cz]
                                  + bias_ref[...]).astype(jnp.bfloat16)
        u = jnp.dot(right_t[...], cots[:, lanes],
                    preferred_element_type=jnp.float32).astype(jnp.bfloat16)
        for q in range(2):
            rows = pl.ds(pl.multiple_of((2 * p + q) * SEQS, 16), SEQS)
            for b in range(HIDDEN):
                v[rows, b * cz:(b + 1) * cz] = u[
                    b * SEQS:(b + 1) * SEQS, q * cz:(q + 1) * cz]

    lg_ref[...] = jnp.dot(v[...], wt_ref[...], preferred_element_type=jnp.float32) * scale
    total[...] += lax.dot_general(z[...], cots[...], (((1,), (1,)), ((), ())),
                                  preferred_element_type=jnp.float32)

    @pl.when(step == pl.num_programs(0) - 1)
    def _():
        rg_ref[...] = (total[...] * scale).T


def pair_blocks(left, right, w, wt, bias, cot):
    rows, cols, cz = cot.shape
    inner = HIDDEN * SEQS
    whole = lambda shape: pl.BlockSpec(shape, lambda i: (0,) * len(shape))
    flops = 2 * rows * (3 * cols * inner * cz + 2 * inner * HIDDEN * cz)
    return pl.pallas_call(
        pair_kernel,
        grid=(rows // BLOCK,),
        in_specs=[
            pl.BlockSpec((BLOCK * SEQS, HIDDEN), lambda i: (i, 0)),
            whole((cols, inner)),
            whole((HIDDEN, HIDDEN * cz)),
            whole((HIDDEN * cz, HIDDEN)),
            whole((1, cz)),
            pl.BlockSpec((BLOCK, cols, cz), lambda i: (i, 0, 0)),
        ],
        out_specs=[
            pl.BlockSpec((BLOCK, cols, cz), lambda i: (i, 0, 0)),
            pl.BlockSpec((BLOCK * SEQS, HIDDEN), lambda i: (i, 0)),
            whole((cols, inner)),
        ],
        out_shape=[
            jax.ShapeDtypeStruct((rows, cols, cz), jnp.bfloat16),
            jax.ShapeDtypeStruct((rows * SEQS, HIDDEN), jnp.float32),
            jax.ShapeDtypeStruct((cols, inner), jnp.float32),
        ],
        scratch_shapes=[
            pltpu.VMEM((inner, cols), jnp.bfloat16),
            pltpu.VMEM((inner, BLOCK * cz), jnp.bfloat16),
            pltpu.VMEM((BLOCK * SEQS, HIDDEN * cz), jnp.bfloat16),
            pltpu.VMEM((cols, BLOCK * cz), jnp.bfloat16),
            pltpu.VMEM((inner, cols), jnp.float32),
        ],
        compiler_params=pltpu.CompilerParams(
            dimension_semantics=("arbitrary",), vmem_limit_bytes=52 * 2**20),
        cost_estimate=pl.CostEstimate(
            flops=flops, bytes_accessed=4 * rows * cols * cz, transcendentals=0),
    )(left, right, w, wt, bias, cot)


def split_dot(x, weight):
    high = x.astype(jnp.bfloat16)
    low = (x - high.astype(jnp.float32)).astype(jnp.bfloat16)
    both = jnp.concatenate([high, low], axis=-1)
    return jnp.dot(both, jnp.concatenate([weight, weight], axis=0),
                   preferred_element_type=jnp.float32)


def shards(row_size, col_size, features, factor, shift, w_first, w_second,
           w_out, bias, cot):
    rows = features.shape[0]
    col = lax.axis_index("col")
    x = features.astype(jnp.float32).reshape(rows, SEQS, CHANNELS)
    center = x - jnp.mean(x, axis=-1, keepdims=True)
    inverse = lax.rsqrt(jnp.mean(center * center, axis=-1, keepdims=True) + 1e-05)
    standard = center * inverse
    normed = (standard * factor + shift).astype(jnp.bfloat16)
    right = jnp.einsum("isc,ch->ihs", normed, w_second,
                       preferred_element_type=jnp.float32).astype(jnp.bfloat16)
    right_all = lax.all_gather(right.reshape(rows, HIDDEN * SEQS), "row", axis=0, tiled=True)
    left = jnp.einsum("isc,ch->ish", normed, w_first,
                      preferred_element_type=jnp.float32).astype(jnp.bfloat16)
    cols = right_all.shape[0] // col_size
    right_use = lax.dynamic_slice_in_dim(right_all, col * cols, cols, 0)
    cz = w_out.shape[1]
    w = w_out.reshape(HIDDEN, HIDDEN * cz)
    wt = w.T
    delta, lg, rg = pair_blocks(left.reshape(rows * SEQS, HIDDEN), right_use, w, wt,
                                bias.reshape(1, cz), cot)
    half = rows // col_size
    lg = lax.psum_scatter(lg, "col", scatter_dimension=0, tiled=True)
    rg = lax.psum_scatter(rg, "row", scatter_dimension=0, tiled=True)
    moves = []
    for r in range(row_size):
        for c in range(col_size):
            chunk = c * row_size + r
            moves.append((r * col_size + c, chunk))
    rg = lax.ppermute(rg, ("row", "col"), moves)
    rg = rg.reshape(half, HIDDEN, SEQS).transpose(0, 2, 1).reshape(half * SEQS, HIDDEN)
    d = split_dot(jnp.concatenate([lg, rg], axis=-1),
                  jnp.concatenate([w_first.T, w_second.T], axis=0))
    e = d.reshape(half, SEQS, CHANNELS) * factor
    std = lax.dynamic_slice_in_dim(standard, col * half, half, 0)
    inv = lax.dynamic_slice_in_dim(inverse, col * half, half, 0)
    grad = inv * (e - jnp.mean(e, axis=-1, keepdims=True)
                  - std * jnp.mean(e * std, axis=-1, keepdims=True))
    grad = grad.astype(jnp.bfloat16).reshape(half, SEQS * CHANNELS)
    grad = lax.all_gather(grad, "col", axis=0, tiled=True)
    return delta, grad


def solution(mesh):
    in_specs = (P(("group", "row"), None), P(), P(), P(), P(), P(), P(),
                P(("group", "row"), "col", None))
    out_specs = (P(("group", "row"), "col", None), P(("group", "row"), None))
    body = functools.partial(shards, mesh.shape["row"], mesh.shape["col"])
    return jax.shard_map(body, mesh=mesh, in_specs=in_specs, out_specs=out_specs,
                         check_vma=False)
```

```python
import functools

import jax
import jax.numpy as jnp
from jax import lax
from jax.experimental import pallas as pl
from jax.experimental.pallas import tpu as pltpu
from jax.sharding import PartitionSpec as P

SEQS = 48
CHANNELS = 64
HIDDEN = 32
BLOCK = 8


def pair_kernel(row_size, col_size, left_ref, right_ref, w_ref, wt_ref, bias_ref, cot_hbm,
                out_hbm, lg_ref, rg_ref,
                right_use, right_t, z, v, cots, total, outs, rg_send, rg_recv,
                lg_send, lg_recv, cot_sem, out_sem, own_sem, gather_send, gather_recv,
                rg_send_sem, rg_recv_sem, lg_send_sem, lg_recv_sem):
    rows, cols, cz = cot_hbm.shape
    blocks = rows // BLOCK
    half_blocks = blocks // col_size
    half = rows // col_size
    owners = row_size // col_size
    scale = 1.0 / SEQS
    row = lax.axis_index("row")
    col = lax.axis_index("col")
    me = row * col_size + col
    devices = row_size * col_size
    home = row // owners
    slot = lax.rem(row, owners)

    def block_rows(index):
        return pl.ds(pl.multiple_of(index * rows, rows), rows)

    def cot_copy(i):
        at = lax.rem(i, BLOCK)
        return pltpu.make_async_copy(
            cot_hbm.at[i],
            cots.at[i // BLOCK, :, pl.ds(pl.multiple_of(at * cz, cz), cz)],
            cot_sem.at[i])

    @pl.loop(0, rows)
    def _(i):
        cot_copy(i).start()

    barrier = pltpu.get_barrier_semaphore()

    @pl.loop(1, devices)
    def _(d):
        other = lax.rem(me + d, devices)
        pl.semaphore_signal(
            barrier, inc=1,
            device_id={"row": other // col_size, "col": lax.rem(other, col_size)},
            device_id_type=pl.DeviceIdType.MESH)
    pl.semaphore_wait(barrier, devices - 1)

    def gather_copy(d):
        target = lax.rem(row + d, row_size)
        return pltpu.make_async_remote_copy(
            src_ref=right_ref, dst_ref=right_use.at[block_rows(slot)],
            send_sem=gather_send.at[d], recv_sem=gather_recv.at[slot],
            device_id={"row": target, "col": home},
            device_id_type=pl.DeviceIdType.MESH)

    def sends(d):
        return lax.rem(lax.rem(row + d, row_size), col_size) == col

    @pl.loop(1, row_size)
    def _(d):
        @pl.when(sends(d))
        def _():
            gather_copy(d).start()

    own_copy = pltpu.make_async_copy(right_ref, right_use.at[block_rows(slot)], own_sem)

    @pl.when(home == col)
    def _():
        own_copy.start()

    total[...] = jnp.zeros_like(total)
    group = 4

    @pl.loop(0, blocks)
    def _(blk):
        lefts = left_ref[pl.ds(pl.multiple_of(blk * BLOCK * SEQS, BLOCK * SEQS), BLOCK * SEQS), :]

        @pl.loop(0, HIDDEN // group)
        def _(g):
            lanes = pl.ds(pl.multiple_of(g * group * cz, group * cz), group * cz)
            part = jnp.dot(lefts, w_ref[:, lanes],
                           preferred_element_type=jnp.float32).astype(jnp.bfloat16)
            for b in range(group):
                at = pl.ds(pl.multiple_of((g * group + b) * SEQS, SEQS), SEQS)
                for i in range(BLOCK):
                    z[blk, at, i * cz:(i + 1) * cz] = part[
                        i * SEQS:(i + 1) * SEQS, b * cz:(b + 1) * cz]

        @pl.loop(0, BLOCK)
        def _(i):
            cot_copy(blk * BLOCK + i).wait()

        total[...] += lax.dot_general(z[blk], cots[blk], (((1,), (1,)), ((), ())),
                                      preferred_element_type=jnp.float32)

    rg_send[...] = (total[...] * scale).T.astype(jnp.bfloat16)

    def rg_rows(q):
        return pl.ds(pl.multiple_of(q * half, half), half)

    def rg_copy(d):
        q = lax.rem(row + d, row_size)
        target = col * row_size + q
        copy = pltpu.make_async_remote_copy(
            src_ref=rg_send.at[rg_rows(q)], dst_ref=rg_recv.at[row],
            send_sem=rg_send_sem.at[d], recv_sem=rg_recv_sem.at[row],
            device_id={"row": target // col_size, "col": lax.rem(target, col_size)},
            device_id_type=pl.DeviceIdType.MESH)
        return q, target != me, copy

    @pl.loop(0, row_size)
    def _(d):
        q, away, copy = rg_copy(d)

        @pl.when(away)
        def _():
            copy.start()

        @pl.when(jnp.logical_not(away))
        def _():
            rg_recv[row] = rg_send[rg_rows(q), :]

    @pl.when(home == col)
    def _():
        own_copy.wait()

    @pl.loop(0, owners)
    def _(k):
        @pl.when(col * owners + k != row)
        def _():
            pltpu.make_async_remote_copy(
                src_ref=right_ref, dst_ref=right_use.at[block_rows(k)],
                send_sem=gather_send.at[0], recv_sem=gather_recv.at[k],
                device_id={"row": row, "col": col},
                device_id_type=pl.DeviceIdType.MESH).wait_recv()

    right_t[...] = right_use[...].T

    def out_copy(blk, at):
        return pltpu.make_async_copy(
            outs.at[at],
            out_hbm.at[pl.ds(pl.multiple_of(blk * BLOCK, BLOCK), BLOCK)], out_sem.at[at])

    def lg_copy(t):
        return pltpu.make_async_remote_copy(
            src_ref=lg_send.at[t], dst_ref=lg_recv.at[t],
            send_sem=lg_send_sem.at[t], recv_sem=lg_recv_sem.at[t],
            device_id={"row": row, "col": 1 - col},
            device_id_type=pl.DeviceIdType.MESH)

    @pl.loop(0, blocks)
    def _(t):
        blk = lax.rem(t + (1 - col) * half_blocks, blocks)
        at = lax.rem(t, 2)

        @pl.when(t >= 2)
        def _():
            out_copy(blk, at).wait()

        @pl.loop(0, BLOCK // 2)
        def _(p):
            lanes = pl.ds(pl.multiple_of(p * 2 * cz, 2 * cz), 2 * cz)
            res = jnp.dot(right_use[...], z[blk, :, lanes],
                          preferred_element_type=jnp.float32) * scale
            for q in range(2):
                outs[at, 2 * p + q] = (res[:, q * cz:(q + 1) * cz]
                                       + bias_ref[...]).astype(jnp.bfloat16)
            u = jnp.dot(right_t[...], cots[blk, :, lanes],
                        preferred_element_type=jnp.float32).astype(jnp.bfloat16)
            for q in range(2):
                to = pl.ds(pl.multiple_of((2 * p + q) * SEQS, SEQS), SEQS)
                for b in range(HIDDEN):
                    v[to, b * cz:(b + 1) * cz] = u[
                        b * SEQS:(b + 1) * SEQS, q * cz:(q + 1) * cz]

        out_copy(blk, at).start()
        lg = jnp.dot(v[...], wt_ref[...], preferred_element_type=jnp.float32) * scale

        @pl.when(t < half_blocks)
        def _():
            lg_send[t] = lg
            lg_copy(t).start()

        @pl.when(t >= half_blocks)
        def _():
            lg_ref[t - half_blocks] = lg

    @pl.loop(0, half_blocks)
    def _(t):
        lg_copy(t).wait_recv()
        lg_ref[t] += lg_recv[t]

    for at in range(2):
        out_copy(0, at).wait()

    @pl.loop(0, row_size)
    def _(k):
        source = k * col_size + home

        @pl.when(source != me)
        def _():
            pltpu.make_async_remote_copy(
                src_ref=rg_send.at[rg_rows(0)], dst_ref=rg_recv.at[k],
                send_sem=rg_send_sem.at[0], recv_sem=rg_recv_sem.at[k],
                device_id={"row": row, "col": col},
                device_id_type=pl.DeviceIdType.MESH).wait_recv()

    summed = rg_recv[0].astype(jnp.float32)
    for k in range(1, row_size):
        summed = summed + rg_recv[k].astype(jnp.float32)
    rg_ref[...] = summed

    @pl.loop(1, row_size)
    def _(d):
        @pl.when(sends(d))
        def _():
            gather_copy(d).wait_send()

    @pl.loop(0, row_size)
    def _(d):
        q, away, copy = rg_copy(d)

        @pl.when(away)
        def _():
            copy.wait_send()

    @pl.loop(0, half_blocks)
    def _(t):
        lg_copy(t).wait_send()


def pair_blocks(row_size, col_size, left, right, w, wt, bias, cot):
    rows, cols, cz = cot.shape
    inner = HIDDEN * SEQS
    blocks = rows // BLOCK
    half_blocks = blocks // col_size
    half = rows // col_size
    flops = 2 * rows * (3 * cols * inner * cz + 2 * inner * HIDDEN * cz)
    vmem = pl.BlockSpec(memory_space=pltpu.VMEM)
    hbm = pl.BlockSpec(memory_space=pl.ANY)
    dma = pltpu.SemaphoreType.DMA
    return pl.pallas_call(
        functools.partial(pair_kernel, row_size, col_size),
        in_specs=[vmem, vmem, vmem, vmem, vmem, hbm],
        out_specs=[hbm, vmem, vmem],
        out_shape=[
            jax.ShapeDtypeStruct((rows, cols, cz), jnp.bfloat16),
            jax.ShapeDtypeStruct((half_blocks, BLOCK * SEQS, HIDDEN), jnp.float32),
            jax.ShapeDtypeStruct((half, inner), jnp.float32),
        ],
        scratch_shapes=[
            pltpu.VMEM((cols, inner), jnp.bfloat16),
            pltpu.VMEM((inner, cols), jnp.bfloat16),
            pltpu.VMEM((blocks, inner, BLOCK * cz), jnp.bfloat16),
            pltpu.VMEM((BLOCK * SEQS, HIDDEN * cz), jnp.bfloat16),
            pltpu.VMEM((blocks, cols, BLOCK * cz), jnp.bfloat16),
            pltpu.VMEM((inner, cols), jnp.float32),
            pltpu.VMEM((2, BLOCK, cols, cz), jnp.bfloat16),
            pltpu.VMEM((cols, inner), jnp.bfloat16),
            pltpu.VMEM((row_size, half, inner), jnp.bfloat16),
            pltpu.VMEM((half_blocks, BLOCK * SEQS, HIDDEN), jnp.float32),
            pltpu.VMEM((half_blocks, BLOCK * SEQS, HIDDEN), jnp.float32),
            dma((rows,)), dma((2,)), dma,
            dma((row_size,)), dma((row_size // col_size,)),
            dma((row_size,)), dma((row_size,)),
            dma((half_blocks,)), dma((half_blocks,)),
        ],
        compiler_params=pltpu.CompilerParams(
            collective_id=0, has_side_effects=True, vmem_limit_bytes=62 * 2**20),
        cost_estimate=pl.CostEstimate(
            flops=flops, bytes_accessed=4 * rows * cols * cz, transcendentals=0),
    )(left, right, w, wt, bias, cot)


def split_dot(x, weight):
    high = x.astype(jnp.bfloat16)
    low = (x - high.astype(jnp.float32)).astype(jnp.bfloat16)
    both = jnp.concatenate([high, low], axis=-1)
    return jnp.dot(both, jnp.concatenate([weight, weight], axis=0),
                   preferred_element_type=jnp.float32)


def shards(row_size, col_size, features, factor, shift, w_first, w_second,
           w_out, bias, cot):
    rows = features.shape[0]
    col = lax.axis_index("col")
    x = features.astype(jnp.float32).reshape(rows, SEQS, CHANNELS)
    center = x - jnp.mean(x, axis=-1, keepdims=True)
    inverse = lax.rsqrt(jnp.mean(center * center, axis=-1, keepdims=True) + 1e-05)
    standard = center * inverse
    normed = (standard * factor + shift).astype(jnp.bfloat16)
    right = jnp.einsum("isc,ch->ihs", normed, w_second,
                       preferred_element_type=jnp.float32).astype(jnp.bfloat16)
    left = jnp.einsum("isc,ch->ish", normed, w_first,
                      preferred_element_type=jnp.float32).astype(jnp.bfloat16)
    cz = w_out.shape[1]
    w = w_out.reshape(HIDDEN, HIDDEN * cz)
    wt = w.T
    delta, lg, rg = pair_blocks(
        row_size, col_size, left.reshape(rows * SEQS, HIDDEN),
        right.reshape(rows, HIDDEN * SEQS), w, wt, bias.reshape(1, cz), cot)
    half = rows // col_size
    lg = lg.reshape(half * SEQS, HIDDEN)
    rg = rg.reshape(half, HIDDEN, SEQS).transpose(0, 2, 1).reshape(half * SEQS, HIDDEN)
    d = split_dot(jnp.concatenate([lg, rg], axis=-1),
                  jnp.concatenate([w_first.T, w_second.T], axis=0))
    e = d.reshape(half, SEQS, CHANNELS) * factor
    std = lax.dynamic_slice_in_dim(standard, col * half, half, 0)
    inv = lax.dynamic_slice_in_dim(inverse, col * half, half, 0)
    grad = inv * (e - jnp.mean(e, axis=-1, keepdims=True)
                  - std * jnp.mean(e * std, axis=-1, keepdims=True))
    grad = grad.astype(jnp.bfloat16).reshape(half, SEQS * CHANNELS)
    grad = lax.all_gather(grad, "col", axis=0, tiled=True)
    return delta, grad


def solution(mesh):
    in_specs = (P(("group", "row"), None), P(), P(), P(), P(), P(), P(),
                P(("group", "row"), "col", None))
    out_specs = (P(("group", "row"), "col", None), P(("group", "row"), None))
    body = functools.partial(shards, mesh.shape["row"], mesh.shape["col"])
    return jax.shard_map(body, mesh=mesh, in_specs=in_specs, out_specs=out_specs,
                         check_vma=False)
```

```python
import functools

import jax
import jax.numpy as jnp
from jax import lax
from jax.experimental import pallas as pl
from jax.experimental.pallas import tpu as pltpu
from jax.sharding import PartitionSpec as P

SEQS = 48
CHANNELS = 64
HIDDEN = 32
BLOCK = 8
Z_GROUP = 8
U_GROUP = 4


def pair_kernel(row_size, col_size, left_ref, right_ref, w_ref, bias_ref, cot_hbm,
                out_hbm, lg_ref, rg_ref,
                right_use, right_t, z, cots, total, outs, rg_send, rg_recv,
                lg_send, lg_recv, cot_sem, out_sem, own_sem, gather_send, gather_recv,
                rg_send_sem, rg_recv_sem, lg_send_sem, lg_recv_sem):
    rows, cols, cz = cot_hbm.shape
    blocks = rows // BLOCK
    half_blocks = blocks // col_size
    half = rows // col_size
    owners = row_size // col_size
    scale = 1.0 / SEQS
    row = lax.axis_index("row")
    col = lax.axis_index("col")
    me = row * col_size + col
    devices = row_size * col_size
    home = row // owners
    slot = lax.rem(row, owners)

    def block_rows(index):
        return pl.ds(pl.multiple_of(index * rows, rows), rows)

    def cot_copy(i):
        at = lax.rem(i, BLOCK)
        return pltpu.make_async_copy(
            cot_hbm.at[i],
            cots.at[i // BLOCK, :, pl.ds(pl.multiple_of(at * cz, cz), cz)],
            cot_sem.at[i])

    @pl.loop(0, rows)
    def _(i):
        cot_copy(i).start()

    barrier = pltpu.get_barrier_semaphore()

    @pl.loop(1, devices)
    def _(d):
        other = lax.rem(me + d, devices)
        pl.semaphore_signal(
            barrier, inc=1,
            device_id={"row": other // col_size, "col": lax.rem(other, col_size)},
            device_id_type=pl.DeviceIdType.MESH)
    pl.semaphore_wait(barrier, devices - 1)

    def gather_copy(d):
        target = lax.rem(row + d, row_size)
        return pltpu.make_async_remote_copy(
            src_ref=right_ref, dst_ref=right_use.at[block_rows(slot)],
            send_sem=gather_send.at[d], recv_sem=gather_recv.at[slot],
            device_id={"row": target, "col": home},
            device_id_type=pl.DeviceIdType.MESH)

    def sends(d):
        return lax.rem(lax.rem(row + d, row_size), col_size) == col

    @pl.loop(1, row_size)
    def _(d):
        @pl.when(sends(d))
        def _():
            gather_copy(d).start()

    own_copy = pltpu.make_async_copy(right_ref, right_use.at[block_rows(slot)], own_sem)

    @pl.when(home == col)
    def _():
        own_copy.start()

    total[...] = jnp.zeros_like(total)

    @pl.loop(0, blocks)
    def _(blk):
        lefts = left_ref[pl.ds(pl.multiple_of(blk * BLOCK * SEQS, BLOCK * SEQS), BLOCK * SEQS), :]

        for g in range(0, HIDDEN, Z_GROUP):
            part = jnp.dot(lefts, w_ref[:, g * cz:(g + Z_GROUP) * cz],
                           preferred_element_type=jnp.float32).astype(jnp.bfloat16)
            for b in range(Z_GROUP):
                at = (g + b) * SEQS
                for i in range(BLOCK):
                    z[blk, at:at + SEQS, i * cz:(i + 1) * cz] = part[
                        i * SEQS:(i + 1) * SEQS, b * cz:(b + 1) * cz]

        @pl.loop(0, BLOCK)
        def _(i):
            cot_copy(blk * BLOCK + i).wait()

        total[...] += lax.dot_general(z[blk], cots[blk], (((1,), (1,)), ((), ())),
                                      preferred_element_type=jnp.float32)

    rg_send[...] = (total[...] * scale).T.astype(jnp.bfloat16)

    def rg_rows(q):
        return pl.ds(pl.multiple_of(q * half, half), half)

    def rg_copy(d):
        q = lax.rem(row + d, row_size)
        target = col * row_size + q
        copy = pltpu.make_async_remote_copy(
            src_ref=rg_send.at[rg_rows(q)], dst_ref=rg_recv.at[row],
            send_sem=rg_send_sem.at[d], recv_sem=rg_recv_sem.at[row],
            device_id={"row": target // col_size, "col": lax.rem(target, col_size)},
            device_id_type=pl.DeviceIdType.MESH)
        return q, target != me, copy

    @pl.loop(0, row_size)
    def _(d):
        q, away, copy = rg_copy(d)

        @pl.when(away)
        def _():
            copy.start()

        @pl.when(jnp.logical_not(away))
        def _():
            rg_recv[row] = rg_send[rg_rows(q), :]

    @pl.when(home == col)
    def _():
        own_copy.wait()

    @pl.loop(0, owners)
    def _(k):
        @pl.when(col * owners + k != row)
        def _():
            pltpu.make_async_remote_copy(
                src_ref=right_ref, dst_ref=right_use.at[block_rows(k)],
                send_sem=gather_send.at[0], recv_sem=gather_recv.at[k],
                device_id={"row": row, "col": col},
                device_id_type=pl.DeviceIdType.MESH).wait_recv()

    right_t[...] = right_use[...].T

    def out_copy(blk, at):
        return pltpu.make_async_copy(
            outs.at[at],
            out_hbm.at[pl.ds(pl.multiple_of(blk * BLOCK, BLOCK), BLOCK)], out_sem.at[at])

    def lg_copy(t):
        return pltpu.make_async_remote_copy(
            src_ref=lg_send.at[t], dst_ref=lg_recv.at[t],
            send_sem=lg_send_sem.at[t], recv_sem=lg_recv_sem.at[t],
            device_id={"row": row, "col": 1 - col},
            device_id_type=pl.DeviceIdType.MESH)

    @pl.loop(0, blocks)
    def _(t):
        blk = lax.rem(t + (1 - col) * half_blocks, blocks)
        at = lax.rem(t, 2)

        @pl.when(t >= 2)
        def _():
            out_copy(blk, at).wait()

        res = jnp.dot(right_use[...], z[blk], preferred_element_type=jnp.float32) * scale
        for i in range(BLOCK):
            outs[at, i] = (res[:, i * cz:(i + 1) * cz] + bias_ref[...]).astype(jnp.bfloat16)
        out_copy(blk, at).start()

        lg = jnp.zeros((BLOCK * SEQS, HIDDEN), jnp.float32)
        for g in range(0, HIDDEN, U_GROUP):
            u = jnp.dot(right_t[g * SEQS:(g + U_GROUP) * SEQS], cots[blk],
                        preferred_element_type=jnp.float32).astype(jnp.bfloat16)
            u = jnp.concatenate([
                jnp.concatenate([
                    u[b * SEQS:(b + 1) * SEQS, i * cz:(i + 1) * cz]
                    for b in range(U_GROUP)], axis=1)
                for i in range(BLOCK)], axis=0)
            lg = lg + lax.dot_general(
                u, w_ref[:, g * cz:(g + U_GROUP) * cz], (((1,), (1,)), ((), ())),
                preferred_element_type=jnp.float32)
        lg = lg * scale

        @pl.when(t < half_blocks)
        def _():
            lg_send[t] = lg
            lg_copy(t).start()

        @pl.when(t >= half_blocks)
        def _():
            lg_ref[t - half_blocks] = lg

    @pl.loop(0, half_blocks)
    def _(t):
        lg_copy(t).wait_recv()
        lg_ref[t] += lg_recv[t]

    for at in range(2):
        out_copy(0, at).wait()

    @pl.loop(0, row_size)
    def _(k):
        source = k * col_size + home

        @pl.when(source != me)
        def _():
            pltpu.make_async_remote_copy(
                src_ref=rg_send.at[rg_rows(0)], dst_ref=rg_recv.at[k],
                send_sem=rg_send_sem.at[0], recv_sem=rg_recv_sem.at[k],
                device_id={"row": row, "col": col},
                device_id_type=pl.DeviceIdType.MESH).wait_recv()

    summed = rg_recv[0].astype(jnp.float32)
    for k in range(1, row_size):
        summed = summed + rg_recv[k].astype(jnp.float32)
    rg_ref[...] = summed

    @pl.loop(1, row_size)
    def _(d):
        @pl.when(sends(d))
        def _():
            gather_copy(d).wait_send()

    @pl.loop(0, row_size)
    def _(d):
        q, away, copy = rg_copy(d)

        @pl.when(away)
        def _():
            copy.wait_send()

    @pl.loop(0, half_blocks)
    def _(t):
        lg_copy(t).wait_send()


def pair_blocks(row_size, col_size, left, right, w, bias, cot):
    rows, cols, cz = cot.shape
    inner = HIDDEN * SEQS
    blocks = rows // BLOCK
    half_blocks = blocks // col_size
    half = rows // col_size
    flops = 2 * rows * (3 * cols * inner * cz + 2 * inner * HIDDEN * cz)
    vmem = pl.BlockSpec(memory_space=pltpu.VMEM)
    hbm = pl.BlockSpec(memory_space=pl.ANY)
    dma = pltpu.SemaphoreType.DMA
    return pl.pallas_call(
        functools.partial(pair_kernel, row_size, col_size),
        in_specs=[vmem, vmem, vmem, vmem, hbm],
        out_specs=[hbm, vmem, vmem],
        out_shape=[
            jax.ShapeDtypeStruct((rows, cols, cz), jnp.bfloat16),
            jax.ShapeDtypeStruct((half_blocks, BLOCK * SEQS, HIDDEN), jnp.float32),
            jax.ShapeDtypeStruct((half, inner), jnp.float32),
        ],
        scratch_shapes=[
            pltpu.VMEM((cols, inner), jnp.bfloat16),
            pltpu.VMEM((inner, cols), jnp.bfloat16),
            pltpu.VMEM((blocks, inner, BLOCK * cz), jnp.bfloat16),
            pltpu.VMEM((blocks, cols, BLOCK * cz), jnp.bfloat16),
            pltpu.VMEM((inner, cols), jnp.float32),
            pltpu.VMEM((2, BLOCK, cols, cz), jnp.bfloat16),
            pltpu.VMEM((cols, inner), jnp.bfloat16),
            pltpu.VMEM((row_size, half, inner), jnp.bfloat16),
            pltpu.VMEM((half_blocks, BLOCK * SEQS, HIDDEN), jnp.float32),
            pltpu.VMEM((half_blocks, BLOCK * SEQS, HIDDEN), jnp.float32),
            dma((rows,)), dma((2,)), dma,
            dma((row_size,)), dma((row_size // col_size,)),
            dma((row_size,)), dma((row_size,)),
            dma((half_blocks,)), dma((half_blocks,)),
        ],
        compiler_params=pltpu.CompilerParams(
            collective_id=0, has_side_effects=True, vmem_limit_bytes=62 * 2**20),
        cost_estimate=pl.CostEstimate(
            flops=flops, bytes_accessed=4 * rows * cols * cz, transcendentals=0),
    )(left, right, w, bias, cot)


def split_dot(x, weight):
    high = x.astype(jnp.bfloat16)
    low = (x - high.astype(jnp.float32)).astype(jnp.bfloat16)
    both = jnp.concatenate([high, low], axis=-1)
    return jnp.dot(both, jnp.concatenate([weight, weight], axis=0),
                   preferred_element_type=jnp.float32)


def shards(row_size, col_size, features, factor, shift, w_first, w_second,
           w_out, bias, cot):
    rows = features.shape[0]
    col = lax.axis_index("col")
    x = features.astype(jnp.float32).reshape(rows, SEQS, CHANNELS)
    center = x - jnp.mean(x, axis=-1, keepdims=True)
    inverse = lax.rsqrt(jnp.mean(center * center, axis=-1, keepdims=True) + 1e-05)
    standard = center * inverse
    normed = (standard * factor + shift).astype(jnp.bfloat16)
    right = jnp.einsum("isc,ch->ihs", normed, w_second,
                       preferred_element_type=jnp.float32).astype(jnp.bfloat16)
    left = jnp.dot(normed.reshape(rows * SEQS, CHANNELS), w_first,
                   preferred_element_type=jnp.float32).astype(jnp.bfloat16)
    cz = w_out.shape[1]
    w = w_out.reshape(HIDDEN, HIDDEN * cz)
    delta, lg, rg = pair_blocks(
        row_size, col_size, left,
        right.reshape(rows, HIDDEN * SEQS), w, bias.reshape(1, cz), cot)
    half = rows // col_size
    lg = lg.reshape(half * SEQS, HIDDEN)
    rg = rg.reshape(half, HIDDEN, SEQS).transpose(0, 2, 1).reshape(half * SEQS, HIDDEN)
    d = split_dot(jnp.concatenate([lg, rg], axis=-1),
                  jnp.concatenate([w_first.T, w_second.T], axis=0))
    e = d.reshape(half, SEQS, CHANNELS) * factor
    std = lax.dynamic_slice_in_dim(standard, col * half, half, 0)
    inv = lax.dynamic_slice_in_dim(inverse, col * half, half, 0)
    grad = inv * (e - jnp.mean(e, axis=-1, keepdims=True)
                  - std * jnp.mean(e * std, axis=-1, keepdims=True))
    grad = grad.astype(jnp.bfloat16).reshape(half, SEQS * CHANNELS)
    grad = lax.all_gather(grad, "col", axis=0, tiled=True)
    return delta, grad


def solution(mesh):
    in_specs = (P(("group", "row"), None), P(), P(), P(), P(), P(), P(),
                P(("group", "row"), "col", None))
    out_specs = (P(("group", "row"), "col", None), P(("group", "row"), None))
    body = functools.partial(shards, mesh.shape["row"], mesh.shape["col"])
    return jax.shard_map(body, mesh=mesh, in_specs=in_specs, out_specs=out_specs,
                         check_vma=False)
```

```python
import functools

import jax
import jax.numpy as jnp
from jax import lax
from jax.experimental import pallas as pl
from jax.experimental.pallas import tpu as pltpu
from jax.sharding import PartitionSpec as P

SEQS = 48
CHANNELS = 64
HIDDEN = 32
BLOCK = 8
Z_GROUP = 8
U_GROUP = 4


def pair_kernel(row_size, col_size, normed_ref, first_ref, right_ref, w_ref, bias_ref, cot_hbm,
                out_hbm, lg_ref, rg_ref,
                right_use, right_t, z, cots, total, outs, rg_send, rg_recv,
                lg_send, lg_recv, cot_sem, out_sem, own_sem, gather_send, gather_recv,
                rg_send_sem, rg_recv_sem, lg_send_sem, lg_recv_sem):
    rows, cols, cz = cot_hbm.shape
    blocks = rows // BLOCK
    half_blocks = blocks // col_size
    half = rows // col_size
    owners = row_size // col_size
    scale = 1.0 / SEQS
    row = lax.axis_index("row")
    col = lax.axis_index("col")
    me = row * col_size + col
    devices = row_size * col_size
    home = row // owners
    slot = lax.rem(row, owners)

    def block_rows(index):
        return pl.ds(pl.multiple_of(index * rows, rows), rows)

    def cot_copy(i):
        at = lax.rem(i, BLOCK)
        return pltpu.make_async_copy(
            cot_hbm.at[i],
            cots.at[i // BLOCK, :, pl.ds(pl.multiple_of(at * cz, cz), cz)],
            cot_sem.at[i])

    @pl.loop(0, rows)
    def _(i):
        cot_copy(i).start()

    barrier = pltpu.get_barrier_semaphore()

    @pl.loop(1, devices)
    def _(d):
        other = lax.rem(me + d, devices)
        pl.semaphore_signal(
            barrier, inc=1,
            device_id={"row": other // col_size, "col": lax.rem(other, col_size)},
            device_id_type=pl.DeviceIdType.MESH)
    pl.semaphore_wait(barrier, devices - 1)

    def gather_copy(d):
        target = lax.rem(row + d, row_size)
        return pltpu.make_async_remote_copy(
            src_ref=right_ref, dst_ref=right_use.at[block_rows(slot)],
            send_sem=gather_send.at[d], recv_sem=gather_recv.at[slot],
            device_id={"row": target, "col": home},
            device_id_type=pl.DeviceIdType.MESH)

    def sends(d):
        return lax.rem(lax.rem(row + d, row_size), col_size) == col

    @pl.loop(1, row_size)
    def _(d):
        @pl.when(sends(d))
        def _():
            gather_copy(d).start()

    own_copy = pltpu.make_async_copy(right_ref, right_use.at[block_rows(slot)], own_sem)

    @pl.when(home == col)
    def _():
        own_copy.start()

    total[...] = jnp.zeros_like(total)

    @pl.loop(0, blocks)
    def _(blk):
        at = pl.ds(pl.multiple_of(blk * BLOCK * SEQS, BLOCK * SEQS), BLOCK * SEQS)
        lefts = jnp.dot(normed_ref[at, :], first_ref[...],
                        preferred_element_type=jnp.float32).astype(jnp.bfloat16)

        for g in range(0, HIDDEN, Z_GROUP):
            part = jnp.dot(lefts, w_ref[:, g * cz:(g + Z_GROUP) * cz],
                           preferred_element_type=jnp.float32).astype(jnp.bfloat16)
            for b in range(Z_GROUP):
                at = (g + b) * SEQS
                for i in range(BLOCK):
                    z[blk, at:at + SEQS, i * cz:(i + 1) * cz] = part[
                        i * SEQS:(i + 1) * SEQS, b * cz:(b + 1) * cz]

        @pl.loop(0, BLOCK)
        def _(i):
            cot_copy(blk * BLOCK + i).wait()

        total[...] += lax.dot_general(z[blk], cots[blk], (((1,), (1,)), ((), ())),
                                      preferred_element_type=jnp.float32)

    rg_send[...] = (total[...] * scale).T.astype(jnp.bfloat16)

    def rg_rows(q):
        return pl.ds(pl.multiple_of(q * half, half), half)

    def rg_copy(d):
        q = lax.rem(row + d, row_size)
        target = col * row_size + q
        copy = pltpu.make_async_remote_copy(
            src_ref=rg_send.at[rg_rows(q)], dst_ref=rg_recv.at[row],
            send_sem=rg_send_sem.at[d], recv_sem=rg_recv_sem.at[row],
            device_id={"row": target // col_size, "col": lax.rem(target, col_size)},
            device_id_type=pl.DeviceIdType.MESH)
        return q, target != me, copy

    @pl.loop(0, row_size)
    def _(d):
        q, away, copy = rg_copy(d)

        @pl.when(away)
        def _():
            copy.start()

        @pl.when(jnp.logical_not(away))
        def _():
            rg_recv[row] = rg_send[rg_rows(q), :]

    @pl.when(home == col)
    def _():
        own_copy.wait()

    @pl.loop(0, owners)
    def _(k):
        @pl.when(col * owners + k != row)
        def _():
            pltpu.make_async_remote_copy(
                src_ref=right_ref, dst_ref=right_use.at[block_rows(k)],
                send_sem=gather_send.at[0], recv_sem=gather_recv.at[k],
                device_id={"row": row, "col": col},
                device_id_type=pl.DeviceIdType.MESH).wait_recv()

    right_t[...] = right_use[...].T

    def out_copy(blk, at):
        return pltpu.make_async_copy(
            outs.at[at],
            out_hbm.at[pl.ds(pl.multiple_of(blk * BLOCK, BLOCK), BLOCK)], out_sem.at[at])

    def lg_copy(t):
        return pltpu.make_async_remote_copy(
            src_ref=lg_send.at[t], dst_ref=lg_recv.at[t],
            send_sem=lg_send_sem.at[t], recv_sem=lg_recv_sem.at[t],
            device_id={"row": row, "col": 1 - col},
            device_id_type=pl.DeviceIdType.MESH)

    @pl.loop(0, blocks)
    def _(t):
        blk = lax.rem(t + (1 - col) * half_blocks, blocks)
        at = lax.rem(t, 2)

        @pl.when(t >= 2)
        def _():
            out_copy(blk, at).wait()

        res = jnp.dot(right_use[...], z[blk], preferred_element_type=jnp.float32) * scale
        for i in range(BLOCK):
            outs[at, i] = (res[:, i * cz:(i + 1) * cz] + bias_ref[...]).astype(jnp.bfloat16)
        out_copy(blk, at).start()

        lg = jnp.zeros((BLOCK * SEQS, HIDDEN), jnp.float32)
        for g in range(0, HIDDEN, U_GROUP):
            u = jnp.dot(right_t[g * SEQS:(g + U_GROUP) * SEQS], cots[blk],
                        preferred_element_type=jnp.float32).astype(jnp.bfloat16)
            u = jnp.concatenate([
                jnp.concatenate([
                    u[b * SEQS:(b + 1) * SEQS, i * cz:(i + 1) * cz]
                    for b in range(U_GROUP)], axis=1)
                for i in range(BLOCK)], axis=0)
            lg = lg + lax.dot_general(
                u, w_ref[:, g * cz:(g + U_GROUP) * cz], (((1,), (1,)), ((), ())),
                preferred_element_type=jnp.float32)
        lg = lg * scale

        @pl.when(t < half_blocks)
        def _():
            lg_send[t] = lg
            lg_copy(t).start()

        @pl.when(t >= half_blocks)
        def _():
            lg_ref[t - half_blocks] = lg

    @pl.loop(0, half_blocks)
    def _(t):
        lg_copy(t).wait_recv()
        lg_ref[t] += lg_recv[t]

    for at in range(2):
        out_copy(0, at).wait()

    @pl.loop(0, row_size)
    def _(k):
        source = k * col_size + home

        @pl.when(source != me)
        def _():
            pltpu.make_async_remote_copy(
                src_ref=rg_send.at[rg_rows(0)], dst_ref=rg_recv.at[k],
                send_sem=rg_send_sem.at[0], recv_sem=rg_recv_sem.at[k],
                device_id={"row": row, "col": col},
                device_id_type=pl.DeviceIdType.MESH).wait_recv()

    summed = rg_recv[0].astype(jnp.float32)
    for k in range(1, row_size):
        summed = summed + rg_recv[k].astype(jnp.float32)
    rg_ref[...] = summed

    @pl.loop(1, row_size)
    def _(d):
        @pl.when(sends(d))
        def _():
            gather_copy(d).wait_send()

    @pl.loop(0, row_size)
    def _(d):
        q, away, copy = rg_copy(d)

        @pl.when(away)
        def _():
            copy.wait_send()

    @pl.loop(0, half_blocks)
    def _(t):
        lg_copy(t).wait_send()


def pair_blocks(row_size, col_size, normed, first, right, w, bias, cot):
    rows, cols, cz = cot.shape
    inner = HIDDEN * SEQS
    blocks = rows // BLOCK
    half_blocks = blocks // col_size
    half = rows // col_size
    flops = 2 * rows * (3 * cols * inner * cz + 2 * inner * HIDDEN * cz)
    vmem = pl.BlockSpec(memory_space=pltpu.VMEM)
    hbm = pl.BlockSpec(memory_space=pl.ANY)
    dma = pltpu.SemaphoreType.DMA
    return pl.pallas_call(
        functools.partial(pair_kernel, row_size, col_size),
        in_specs=[vmem, vmem, vmem, vmem, vmem, hbm],
        out_specs=[hbm, vmem, vmem],
        out_shape=[
            jax.ShapeDtypeStruct((rows, cols, cz), jnp.bfloat16),
            jax.ShapeDtypeStruct((half_blocks, BLOCK * SEQS, HIDDEN), jnp.float32),
            jax.ShapeDtypeStruct((half, inner), jnp.float32),
        ],
        scratch_shapes=[
            pltpu.VMEM((cols, inner), jnp.bfloat16),
            pltpu.VMEM((inner, cols), jnp.bfloat16),
            pltpu.VMEM((blocks, inner, BLOCK * cz), jnp.bfloat16),
            pltpu.VMEM((blocks, cols, BLOCK * cz), jnp.bfloat16),
            pltpu.VMEM((inner, cols), jnp.float32),
            pltpu.VMEM((2, BLOCK, cols, cz), jnp.bfloat16),
            pltpu.VMEM((cols, inner), jnp.bfloat16),
            pltpu.VMEM((row_size, half, inner), jnp.bfloat16),
            pltpu.VMEM((half_blocks, BLOCK * SEQS, HIDDEN), jnp.float32),
            pltpu.VMEM((half_blocks, BLOCK * SEQS, HIDDEN), jnp.float32),
            dma((rows,)), dma((2,)), dma,
            dma((row_size,)), dma((row_size // col_size,)),
            dma((row_size,)), dma((row_size,)),
            dma((half_blocks,)), dma((half_blocks,)),
        ],
        compiler_params=pltpu.CompilerParams(
            collective_id=0, has_side_effects=True, vmem_limit_bytes=62 * 2**20),
        cost_estimate=pl.CostEstimate(
            flops=flops, bytes_accessed=4 * rows * cols * cz, transcendentals=0),
    )(normed, first, right, w, bias, cot)


def split_dot(x, weight):
    high = x.astype(jnp.bfloat16)
    low = (x - high.astype(jnp.float32)).astype(jnp.bfloat16)
    both = jnp.concatenate([high, low], axis=-1)
    return jnp.dot(both, jnp.concatenate([weight, weight], axis=0),
                   preferred_element_type=jnp.float32)


def shards(row_size, col_size, features, factor, shift, w_first, w_second,
           w_out, bias, cot):
    rows = features.shape[0]
    col = lax.axis_index("col")
    x = features.astype(jnp.float32).reshape(rows, SEQS, CHANNELS)
    center = x - jnp.mean(x, axis=-1, keepdims=True)
    inverse = lax.rsqrt(jnp.mean(center * center, axis=-1, keepdims=True) + 1e-05)
    standard = center * inverse
    normed = (standard * factor + shift).astype(jnp.bfloat16)
    right = jnp.einsum("isc,ch->ihs", normed, w_second,
                       preferred_element_type=jnp.float32).astype(jnp.bfloat16)
    cz = w_out.shape[1]
    w = w_out.reshape(HIDDEN, HIDDEN * cz)
    delta, lg, rg = pair_blocks(
        row_size, col_size, normed.reshape(rows * SEQS, CHANNELS), w_first,
        right.reshape(rows, HIDDEN * SEQS), w, bias.reshape(1, cz), cot)
    half = rows // col_size
    lg = lg.reshape(half * SEQS, HIDDEN)
    rg = rg.reshape(half, HIDDEN, SEQS).transpose(0, 2, 1).reshape(half * SEQS, HIDDEN)
    d = split_dot(jnp.concatenate([lg, rg], axis=-1),
                  jnp.concatenate([w_first.T, w_second.T], axis=0))
    e = d.reshape(half, SEQS, CHANNELS) * factor
    std = lax.dynamic_slice_in_dim(standard, col * half, half, 0)
    inv = lax.dynamic_slice_in_dim(inverse, col * half, half, 0)
    grad = inv * (e - jnp.mean(e, axis=-1, keepdims=True)
                  - std * jnp.mean(e * std, axis=-1, keepdims=True))
    grad = grad.astype(jnp.bfloat16).reshape(half, SEQS * CHANNELS)
    grad = lax.all_gather(grad, "col", axis=0, tiled=True)
    return delta, grad


def solution(mesh):
    in_specs = (P(("group", "row"), None), P(), P(), P(), P(), P(), P(),
                P(("group", "row"), "col", None))
    out_specs = (P(("group", "row"), "col", None), P(("group", "row"), None))
    body = functools.partial(shards, mesh.shape["row"], mesh.shape["col"])
    return jax.shard_map(body, mesh=mesh, in_specs=in_specs, out_specs=out_specs,
                         check_vma=False)
```

```python
import functools

import jax
import jax.numpy as jnp
from jax import lax
from jax.experimental import pallas as pl
from jax.experimental.pallas import tpu as pltpu
from jax.sharding import PartitionSpec as P

SEQS = 48
CHANNELS = 64
HIDDEN = 32
BLOCK = 8
Z_GROUP = 8
U_GROUP = 4


def pair_kernel(row_size, col_size, normed_ref, first_ref, right_ref, w_ref, bias_ref, cot_hbm,
                out_hbm, lg_ref, rg_ref,
                right_use, right_t, z, cots, total, outs, rg_send, rg_recv,
                lg_send, lg_recv, cot_sem, out_sem, own_sem, gather_send, gather_recv,
                rg_send_sem, rg_recv_sem, lg_send_sem, lg_recv_sem):
    rows, cols, cz = cot_hbm.shape
    blocks = rows // BLOCK
    half_blocks = blocks // col_size
    half = rows // col_size
    owners = row_size // col_size
    scale = 1.0 / SEQS
    row = lax.axis_index("row")
    col = lax.axis_index("col")
    me = row * col_size + col
    devices = row_size * col_size
    home = row // owners
    slot = lax.rem(row, owners)

    def block_rows(index):
        return pl.ds(pl.multiple_of(index * rows, rows), rows)

    def cot_copy(i):
        at = lax.rem(i, BLOCK)
        return pltpu.make_async_copy(
            cot_hbm.at[i],
            cots.at[i // BLOCK, :, pl.ds(pl.multiple_of(at * cz, cz), cz)],
            cot_sem.at[i])

    @pl.loop(0, rows)
    def _(i):
        cot_copy(i).start()

    barrier = pltpu.get_barrier_semaphore()

    @pl.loop(1, devices)
    def _(d):
        other = lax.rem(me + d, devices)
        pl.semaphore_signal(
            barrier, inc=1,
            device_id={"row": other // col_size, "col": lax.rem(other, col_size)},
            device_id_type=pl.DeviceIdType.MESH)
    pl.semaphore_wait(barrier, devices - 1)

    def gather_copy(d):
        target = lax.rem(row + d, row_size)
        return pltpu.make_async_remote_copy(
            src_ref=right_ref, dst_ref=right_use.at[block_rows(slot)],
            send_sem=gather_send.at[d], recv_sem=gather_recv.at[slot],
            device_id={"row": target, "col": home},
            device_id_type=pl.DeviceIdType.MESH)

    def sends(d):
        return lax.rem(lax.rem(row + d, row_size), col_size) == col

    @pl.loop(1, row_size)
    def _(d):
        @pl.when(sends(d))
        def _():
            gather_copy(d).start()

    own_copy = pltpu.make_async_copy(right_ref, right_use.at[block_rows(slot)], own_sem)

    @pl.when(home == col)
    def _():
        own_copy.start()

    total[...] = jnp.zeros_like(total)

    @pl.loop(0, blocks)
    def _(blk):
        at = pl.ds(pl.multiple_of(blk * BLOCK * SEQS, BLOCK * SEQS), BLOCK * SEQS)
        lefts = jnp.dot(normed_ref[at, :], first_ref[...],
                        preferred_element_type=jnp.float32).astype(jnp.bfloat16)

        for g in range(0, HIDDEN, Z_GROUP):
            part = jnp.dot(lefts, w_ref[:, g * cz:(g + Z_GROUP) * cz],
                           preferred_element_type=jnp.float32).astype(jnp.bfloat16)
            for b in range(Z_GROUP):
                at = (g + b) * SEQS
                for i in range(BLOCK):
                    z[blk, at:at + SEQS, i * cz:(i + 1) * cz] = part[
                        i * SEQS:(i + 1) * SEQS, b * cz:(b + 1) * cz]

        @pl.loop(0, BLOCK)
        def _(i):
            cot_copy(blk * BLOCK + i).wait()

        total[...] += lax.dot_general(z[blk], cots[blk], (((1,), (1,)), ((), ())),
                                      preferred_element_type=jnp.float32)

    rg_send[...] = (total[...] * scale).T.astype(jnp.bfloat16)

    def rg_rows(q):
        return pl.ds(pl.multiple_of(q * half, half), half)

    def rg_copy(d):
        q = lax.rem(row + d, row_size)
        target = col * row_size + q
        copy = pltpu.make_async_remote_copy(
            src_ref=rg_send.at[rg_rows(q)], dst_ref=rg_recv.at[row],
            send_sem=rg_send_sem.at[d], recv_sem=rg_recv_sem.at[row],
            device_id={"row": target // col_size, "col": lax.rem(target, col_size)},
            device_id_type=pl.DeviceIdType.MESH)
        return q, target != me, copy

    @pl.loop(0, row_size)
    def _(d):
        q, away, copy = rg_copy(d)

        @pl.when(away)
        def _():
            copy.start()

        @pl.when(jnp.logical_not(away))
        def _():
            rg_recv[row] = rg_send[rg_rows(q), :]

    @pl.when(home == col)
    def _():
        own_copy.wait()

    @pl.loop(0, owners)
    def _(k):
        @pl.when(col * owners + k != row)
        def _():
            pltpu.make_async_remote_copy(
                src_ref=right_ref, dst_ref=right_use.at[block_rows(k)],
                send_sem=gather_send.at[0], recv_sem=gather_recv.at[k],
                device_id={"row": row, "col": col},
                device_id_type=pl.DeviceIdType.MESH).wait_recv()

    right_t[...] = right_use[...].T

    def out_copy(blk, at):
        return pltpu.make_async_copy(
            outs.at[at],
            out_hbm.at[pl.ds(pl.multiple_of(blk * BLOCK, BLOCK), BLOCK)], out_sem.at[at])

    def lg_copy(t):
        return pltpu.make_async_remote_copy(
            src_ref=lg_send.at[t], dst_ref=lg_recv.at[t],
            send_sem=lg_send_sem.at[t], recv_sem=lg_recv_sem.at[t],
            device_id={"row": row, "col": 1 - col},
            device_id_type=pl.DeviceIdType.MESH)

    @pl.loop(0, blocks)
    def _(t):
        blk = lax.rem(t + (1 - col) * half_blocks, blocks)
        at = lax.rem(t, 2)

        @pl.when(t >= 2)
        def _():
            out_copy(blk, at).wait()

        res = jnp.dot(right_use[...], z[blk], preferred_element_type=jnp.float32) * scale
        for i in range(BLOCK):
            outs[at, i] = (res[:, i * cz:(i + 1) * cz] + bias_ref[...]).astype(jnp.bfloat16)
        out_copy(blk, at).start()

        lg = jnp.zeros((BLOCK * SEQS, HIDDEN), jnp.float32)
        for g in range(0, HIDDEN, U_GROUP):
            u = jnp.dot(right_t[g * SEQS:(g + U_GROUP) * SEQS], cots[blk],
                        preferred_element_type=jnp.float32).astype(jnp.bfloat16)
            u = jnp.concatenate([
                jnp.concatenate([
                    u[b * SEQS:(b + 1) * SEQS, i * cz:(i + 1) * cz]
                    for b in range(U_GROUP)], axis=1)
                for i in range(BLOCK)], axis=0)
            lg = lg + lax.dot_general(
                u, w_ref[:, g * cz:(g + U_GROUP) * cz], (((1,), (1,)), ((), ())),
                preferred_element_type=jnp.float32)
        lg = lg * scale

        @pl.when(t < half_blocks)
        def _():
            lg_send[t] = lg
            lg_copy(t).start()

        @pl.when(t >= half_blocks)
        def _():
            lg_ref[t - half_blocks] = lg

    @pl.loop(0, half_blocks)
    def _(t):
        lg_copy(t).wait_recv()
        lg_ref[t] += lg_recv[t]

    for at in range(2):
        out_copy(0, at).wait()

    @pl.loop(0, row_size)
    def _(k):
        source = k * col_size + home

        @pl.when(source != me)
        def _():
            pltpu.make_async_remote_copy(
                src_ref=rg_send.at[rg_rows(0)], dst_ref=rg_recv.at[k],
                send_sem=rg_send_sem.at[0], recv_sem=rg_recv_sem.at[k],
                device_id={"row": row, "col": col},
                device_id_type=pl.DeviceIdType.MESH).wait_recv()

    summed = rg_recv[0].astype(jnp.float32)
    for k in range(1, row_size):
        summed = summed + rg_recv[k].astype(jnp.float32)
    rg_ref[...] = summed

    @pl.loop(1, row_size)
    def _(d):
        @pl.when(sends(d))
        def _():
            gather_copy(d).wait_send()

    @pl.loop(0, row_size)
    def _(d):
        q, away, copy = rg_copy(d)

        @pl.when(away)
        def _():
            copy.wait_send()

    @pl.loop(0, half_blocks)
    def _(t):
        lg_copy(t).wait_send()


def pair_blocks(row_size, col_size, normed, first, right, w, bias, cot):
    rows, cols, cz = cot.shape
    inner = HIDDEN * SEQS
    blocks = rows // BLOCK
    half_blocks = blocks // col_size
    half = rows // col_size
    flops = 2 * rows * (3 * cols * inner * cz + 2 * inner * HIDDEN * cz)
    vmem = pl.BlockSpec(memory_space=pltpu.VMEM)
    hbm = pl.BlockSpec(memory_space=pl.ANY)
    dma = pltpu.SemaphoreType.DMA
    return pl.pallas_call(
        functools.partial(pair_kernel, row_size, col_size),
        in_specs=[vmem, vmem, vmem, vmem, vmem, hbm],
        out_specs=[hbm, vmem, vmem],
        out_shape=[
            jax.ShapeDtypeStruct((rows, cols, cz), jnp.bfloat16),
            jax.ShapeDtypeStruct((half_blocks, BLOCK * SEQS, HIDDEN), jnp.float32),
            jax.ShapeDtypeStruct((half, inner), jnp.float32),
        ],
        scratch_shapes=[
            pltpu.VMEM((cols, inner), jnp.bfloat16),
            pltpu.VMEM((inner, cols), jnp.bfloat16),
            pltpu.VMEM((blocks, inner, BLOCK * cz), jnp.bfloat16),
            pltpu.VMEM((blocks, cols, BLOCK * cz), jnp.bfloat16),
            pltpu.VMEM((inner, cols), jnp.float32),
            pltpu.VMEM((2, BLOCK, cols, cz), jnp.bfloat16),
            pltpu.VMEM((cols, inner), jnp.bfloat16),
            pltpu.VMEM((row_size, half, inner), jnp.bfloat16),
            pltpu.VMEM((half_blocks, BLOCK * SEQS, HIDDEN), jnp.float32),
            pltpu.VMEM((half_blocks, BLOCK * SEQS, HIDDEN), jnp.float32),
            dma((rows,)), dma((2,)), dma,
            dma((row_size,)), dma((row_size // col_size,)),
            dma((row_size,)), dma((row_size,)),
            dma((half_blocks,)), dma((half_blocks,)),
        ],
        compiler_params=pltpu.CompilerParams(
            collective_id=0, has_side_effects=True, vmem_limit_bytes=62 * 2**20),
        cost_estimate=pl.CostEstimate(
            flops=flops, bytes_accessed=4 * rows * cols * cz, transcendentals=0),
    )(normed, first, right, w, bias, cot)


def split_dot(x, weight):
    high = x.astype(jnp.bfloat16)
    low = (x - high.astype(jnp.float32)).astype(jnp.bfloat16)
    both = jnp.concatenate([high, low], axis=-1)
    return jnp.dot(both, jnp.concatenate([weight, weight], axis=0),
                   preferred_element_type=jnp.float32)


def shards(row_size, col_size, features, factor, shift, w_first, w_second,
           w_out, bias, cot):
    rows = features.shape[0]
    col = lax.axis_index("col")
    x = features.astype(jnp.float32).reshape(rows, SEQS, CHANNELS)
    center = x - jnp.mean(x, axis=-1, keepdims=True)
    inverse = lax.rsqrt(jnp.mean(center * center, axis=-1, keepdims=True) + 1e-05)
    standard = center * inverse
    normed = (standard * factor + shift).astype(jnp.bfloat16)
    normed, standard, inverse = lax.optimization_barrier((normed, standard, inverse))
    right = jnp.einsum("isc,ch->ihs", normed, w_second,
                       preferred_element_type=jnp.float32).astype(jnp.bfloat16)
    cz = w_out.shape[1]
    w = w_out.reshape(HIDDEN, HIDDEN * cz)
    delta, lg, rg = pair_blocks(
        row_size, col_size, normed.reshape(rows * SEQS, CHANNELS), w_first,
        right.reshape(rows, HIDDEN * SEQS), w, bias.reshape(1, cz), cot)
    half = rows // col_size
    lg = lg.reshape(half * SEQS, HIDDEN)
    rg = rg.reshape(half, HIDDEN, SEQS).transpose(0, 2, 1).reshape(half * SEQS, HIDDEN)
    d = split_dot(jnp.concatenate([lg, rg], axis=-1),
                  jnp.concatenate([w_first.T, w_second.T], axis=0))
    e = d.reshape(half, SEQS, CHANNELS) * factor
    std = lax.dynamic_slice_in_dim(standard, col * half, half, 0)
    inv = lax.dynamic_slice_in_dim(inverse, col * half, half, 0)
    grad = inv * (e - jnp.mean(e, axis=-1, keepdims=True)
                  - std * jnp.mean(e * std, axis=-1, keepdims=True))
    grad = grad.astype(jnp.bfloat16).reshape(half, SEQS * CHANNELS)
    grad = lax.all_gather(grad, "col", axis=0, tiled=True)
    return delta, grad


def solution(mesh):
    in_specs = (P(("group", "row"), None), P(), P(), P(), P(), P(), P(),
                P(("group", "row"), "col", None))
    out_specs = (P(("group", "row"), "col", None), P(("group", "row"), None))
    body = functools.partial(shards, mesh.shape["row"], mesh.shape["col"])
    return jax.shard_map(body, mesh=mesh, in_specs=in_specs, out_specs=out_specs,
                         check_vma=False)
```

```python
import functools

import jax
import jax.numpy as jnp
from jax import lax
from jax.experimental import pallas as pl
from jax.experimental.pallas import tpu as pltpu
from jax.sharding import PartitionSpec as P

SEQS = 48
CHANNELS = 64
HIDDEN = 32
BLOCK = 8
Z_GROUP = 8
U_GROUP = 4


def pair_kernel(row_size, col_size, normed_ref, first_ref, right_ref, w_ref, bias_ref, cot_hbm,
                out_hbm, lg_ref, rg_ref,
                right_use, right_t, z, cots, total, outs, rg_send, rg_recv,
                lg_send, lg_recv, cot_sem, out_sem, own_sem, gather_send, gather_recv,
                rg_send_sem, rg_recv_sem, lg_send_sem, lg_recv_sem):
    rows, cols, cz = cot_hbm.shape
    blocks = rows // BLOCK
    half_blocks = blocks // col_size
    half = rows // col_size
    owners = row_size // col_size
    scale = 1.0 / SEQS
    row = lax.axis_index("row")
    col = lax.axis_index("col")
    me = row * col_size + col
    devices = row_size * col_size
    home = row // owners
    slot = lax.rem(row, owners)

    def block_rows(index):
        return pl.ds(pl.multiple_of(index * rows, rows), rows)

    def cot_copy(i):
        at = lax.rem(i, BLOCK)
        return pltpu.make_async_copy(
            cot_hbm.at[i],
            cots.at[i // BLOCK, :, pl.ds(pl.multiple_of(at * cz, cz), cz)],
            cot_sem.at[i])

    @pl.loop(0, rows)
    def _(i):
        cot_copy(i).start()

    barrier = pltpu.get_barrier_semaphore()

    @pl.loop(1, devices)
    def _(d):
        other = lax.rem(me + d, devices)
        pl.semaphore_signal(
            barrier, inc=1,
            device_id={"row": other // col_size, "col": lax.rem(other, col_size)},
            device_id_type=pl.DeviceIdType.MESH)
    pl.semaphore_wait(barrier, devices - 1)

    def gather_copy(d):
        target = lax.rem(row + d, row_size)
        return pltpu.make_async_remote_copy(
            src_ref=right_ref, dst_ref=right_use.at[block_rows(slot)],
            send_sem=gather_send.at[d], recv_sem=gather_recv.at[slot],
            device_id={"row": target, "col": home},
            device_id_type=pl.DeviceIdType.MESH)

    def sends(d):
        return lax.rem(lax.rem(row + d, row_size), col_size) == col

    @pl.loop(1, row_size)
    def _(d):
        @pl.when(sends(d))
        def _():
            gather_copy(d).start()

    own_copy = pltpu.make_async_copy(right_ref, right_use.at[block_rows(slot)], own_sem)

    @pl.when(home == col)
    def _():
        own_copy.start()

    total[...] = jnp.zeros_like(total)

    @pl.loop(0, blocks)
    def _(blk):
        at = pl.ds(pl.multiple_of(blk * BLOCK * SEQS, BLOCK * SEQS), BLOCK * SEQS)
        lefts = jnp.dot(normed_ref[at, :], first_ref[...],
                        preferred_element_type=jnp.float32).astype(jnp.bfloat16)

        for g in range(0, HIDDEN, Z_GROUP):
            part = jnp.dot(lefts, w_ref[:, g * cz:(g + Z_GROUP) * cz],
                           preferred_element_type=jnp.float32).astype(jnp.bfloat16)
            for b in range(Z_GROUP):
                at = (g + b) * SEQS
                for i in range(BLOCK):
                    z[blk, at:at + SEQS, i * cz:(i + 1) * cz] = part[
                        i * SEQS:(i + 1) * SEQS, b * cz:(b + 1) * cz]

        @pl.loop(0, BLOCK)
        def _(i):
            cot_copy(blk * BLOCK + i).wait()

        total[...] += lax.dot_general(z[blk], cots[blk], (((1,), (1,)), ((), ())),
                                      preferred_element_type=jnp.float32)

    rg_send[...] = (total[...] * scale).T.astype(jnp.bfloat16)

    def rg_rows(q):
        return pl.ds(pl.multiple_of(q * half, half), half)

    def rg_copy(d):
        q = lax.rem(row + d, row_size)
        target = col * row_size + q
        copy = pltpu.make_async_remote_copy(
            src_ref=rg_send.at[rg_rows(q)], dst_ref=rg_recv.at[row],
            send_sem=rg_send_sem.at[d], recv_sem=rg_recv_sem.at[row],
            device_id={"row": target // col_size, "col": lax.rem(target, col_size)},
            device_id_type=pl.DeviceIdType.MESH)
        return q, target != me, copy

    @pl.loop(0, row_size)
    def _(d):
        q, away, copy = rg_copy(d)

        @pl.when(away)
        def _():
            copy.start()

        @pl.when(jnp.logical_not(away))
        def _():
            rg_recv[row] = rg_send[rg_rows(q), :]

    @pl.when(home == col)
    def _():
        own_copy.wait()

    @pl.loop(0, owners)
    def _(k):
        @pl.when(col * owners + k != row)
        def _():
            pltpu.make_async_remote_copy(
                src_ref=right_ref, dst_ref=right_use.at[block_rows(k)],
                send_sem=gather_send.at[0], recv_sem=gather_recv.at[k],
                device_id={"row": row, "col": col},
                device_id_type=pl.DeviceIdType.MESH).wait_recv()

    right_t[...] = right_use[...].T

    def out_copy(blk, at):
        return pltpu.make_async_copy(
            outs.at[at],
            out_hbm.at[pl.ds(pl.multiple_of(blk * BLOCK, BLOCK), BLOCK)], out_sem.at[at])

    def lg_copy(t):
        return pltpu.make_async_remote_copy(
            src_ref=lg_send.at[t], dst_ref=lg_recv.at[t],
            send_sem=lg_send_sem.at[t], recv_sem=lg_recv_sem.at[t],
            device_id={"row": row, "col": 1 - col},
            device_id_type=pl.DeviceIdType.MESH)

    @pl.loop(0, blocks)
    def _(t):
        blk = lax.rem(t + (1 - col) * half_blocks, blocks)
        at = lax.rem(t, 2)

        @pl.when(t >= 2)
        def _():
            out_copy(blk, at).wait()

        res = jnp.dot(right_use[...], z[blk], preferred_element_type=jnp.float32) * scale
        for i in range(BLOCK):
            outs[at, i] = (res[:, i * cz:(i + 1) * cz] + bias_ref[...]).astype(jnp.bfloat16)
        out_copy(blk, at).start()

        lg = jnp.zeros((BLOCK * SEQS, HIDDEN), jnp.float32)
        for g in range(0, HIDDEN, U_GROUP):
            u = jnp.dot(right_t[g * SEQS:(g + U_GROUP) * SEQS], cots[blk],
                        preferred_element_type=jnp.float32).astype(jnp.bfloat16)
            u = jnp.concatenate([
                jnp.concatenate([
                    u[b * SEQS:(b + 1) * SEQS, i * cz:(i + 1) * cz]
                    for b in range(U_GROUP)], axis=1)
                for i in range(BLOCK)], axis=0)
            lg = lg + lax.dot_general(
                u, w_ref[:, g * cz:(g + U_GROUP) * cz], (((1,), (1,)), ((), ())),
                preferred_element_type=jnp.float32)
        lg = lg * scale

        @pl.when(t < half_blocks)
        def _():
            lg_send[t] = lg
            lg_copy(t).start()

        @pl.when(t >= half_blocks)
        def _():
            lg_ref[t - half_blocks] = lg

    @pl.loop(0, half_blocks)
    def _(t):
        lg_copy(t).wait_recv()
        lg_ref[t] += lg_recv[t]

    for at in range(2):
        out_copy(0, at).wait()

    @pl.loop(0, row_size)
    def _(k):
        source = k * col_size + home

        @pl.when(source != me)
        def _():
            pltpu.make_async_remote_copy(
                src_ref=rg_send.at[rg_rows(0)], dst_ref=rg_recv.at[k],
                send_sem=rg_send_sem.at[0], recv_sem=rg_recv_sem.at[k],
                device_id={"row": row, "col": col},
                device_id_type=pl.DeviceIdType.MESH).wait_recv()

    summed = rg_recv[0].astype(jnp.float32)
    for k in range(1, row_size):
        summed = summed + rg_recv[k].astype(jnp.float32)
    rg_ref[...] = summed

    @pl.loop(1, row_size)
    def _(d):
        @pl.when(sends(d))
        def _():
            gather_copy(d).wait_send()

    @pl.loop(0, row_size)
    def _(d):
        q, away, copy = rg_copy(d)

        @pl.when(away)
        def _():
            copy.wait_send()

    @pl.loop(0, half_blocks)
    def _(t):
        lg_copy(t).wait_send()


def pair_blocks(row_size, col_size, normed, first, right, w, bias, cot):
    rows, cols, cz = cot.shape
    inner = HIDDEN * SEQS
    blocks = rows // BLOCK
    half_blocks = blocks // col_size
    half = rows // col_size
    flops = 2 * rows * (3 * cols * inner * cz + 2 * inner * HIDDEN * cz)
    vmem = pl.BlockSpec(memory_space=pltpu.VMEM)
    hbm = pl.BlockSpec(memory_space=pl.ANY)
    dma = pltpu.SemaphoreType.DMA
    return pl.pallas_call(
        functools.partial(pair_kernel, row_size, col_size),
        in_specs=[vmem, vmem, vmem, vmem, vmem, hbm],
        out_specs=[hbm, vmem, vmem],
        out_shape=[
            jax.ShapeDtypeStruct((rows, cols, cz), jnp.bfloat16),
            jax.ShapeDtypeStruct((half_blocks, BLOCK * SEQS, HIDDEN), jnp.float32),
            jax.ShapeDtypeStruct((half, inner), jnp.float32),
        ],
        scratch_shapes=[
            pltpu.VMEM((cols, inner), jnp.bfloat16),
            pltpu.VMEM((inner, cols), jnp.bfloat16),
            pltpu.VMEM((blocks, inner, BLOCK * cz), jnp.bfloat16),
            pltpu.VMEM((blocks, cols, BLOCK * cz), jnp.bfloat16),
            pltpu.VMEM((inner, cols), jnp.float32),
            pltpu.VMEM((2, BLOCK, cols, cz), jnp.bfloat16),
            pltpu.VMEM((cols, inner), jnp.bfloat16),
            pltpu.VMEM((row_size, half, inner), jnp.bfloat16),
            pltpu.VMEM((half_blocks, BLOCK * SEQS, HIDDEN), jnp.float32),
            pltpu.VMEM((half_blocks, BLOCK * SEQS, HIDDEN), jnp.float32),
            dma((rows,)), dma((2,)), dma,
            dma((row_size,)), dma((row_size // col_size,)),
            dma((row_size,)), dma((row_size,)),
            dma((half_blocks,)), dma((half_blocks,)),
        ],
        compiler_params=pltpu.CompilerParams(
            collective_id=0, has_side_effects=True, vmem_limit_bytes=62 * 2**20),
        cost_estimate=pl.CostEstimate(
            flops=flops, bytes_accessed=4 * rows * cols * cz, transcendentals=0),
    )(normed, first, right, w, bias, cot)


def split_dot(x, weight):
    high = x.astype(jnp.bfloat16)
    low = (x - high.astype(jnp.float32)).astype(jnp.bfloat16)
    both = jnp.concatenate([high, low], axis=-1)
    return jnp.dot(both, jnp.concatenate([weight, weight], axis=0),
                   preferred_element_type=jnp.float32)


def shards(row_size, col_size, features, factor, shift, w_first, w_second,
           w_out, bias, cot):
    rows = features.shape[0]
    col = lax.axis_index("col")
    x = features.astype(jnp.float32).reshape(rows, SEQS, CHANNELS)
    center = x - jnp.mean(x, axis=-1, keepdims=True)
    inverse = lax.rsqrt(jnp.mean(center * center, axis=-1, keepdims=True) + 1e-05)
    standard = center * inverse
    normed = (standard * factor + shift).astype(jnp.bfloat16)
    normed, standard, inverse = lax.optimization_barrier((normed, standard, inverse))
    right = jnp.einsum("isc,ch->ihs", normed, w_second,
                       preferred_element_type=jnp.float32).astype(jnp.bfloat16)
    cz = w_out.shape[1]
    w = w_out.reshape(HIDDEN, HIDDEN * cz)
    delta, lg, rg = pair_blocks(
        row_size, col_size, normed.reshape(rows * SEQS, CHANNELS), w_first,
        right.reshape(rows, HIDDEN * SEQS), w, bias.reshape(1, cz), cot)
    half = rows // col_size
    lg = lg.reshape(half * SEQS, HIDDEN)
    rg = rg.reshape(half, HIDDEN, SEQS).transpose(0, 2, 1).reshape(half * SEQS, HIDDEN)
    d = split_dot(lg, w_first.T) + split_dot(rg, w_second.T)
    e = d.reshape(half, SEQS, CHANNELS) * factor
    std = lax.dynamic_slice_in_dim(standard, col * half, half, 0)
    inv = lax.dynamic_slice_in_dim(inverse, col * half, half, 0)
    grad = inv * (e - jnp.mean(e, axis=-1, keepdims=True)
                  - std * jnp.mean(e * std, axis=-1, keepdims=True))
    grad = grad.astype(jnp.bfloat16).reshape(half, SEQS * CHANNELS)
    grad = lax.all_gather(grad, "col", axis=0, tiled=True)
    return delta, grad


def solution(mesh):
    in_specs = (P(("group", "row"), None), P(), P(), P(), P(), P(), P(),
                P(("group", "row"), "col", None))
    out_specs = (P(("group", "row"), "col", None), P(("group", "row"), None))
    body = functools.partial(shards, mesh.shape["row"], mesh.shape["col"])
    return jax.shard_map(body, mesh=mesh, in_specs=in_specs, out_specs=out_specs,
                         check_vma=False)
```
